32 devices in a mesh: groups: 2 (over y), blocks: 4 (over z), pairs: 2 (over x), dims: 2 (over core).
Axes of the slice: x: 2, y: 2, z: 4, core: 2. Of those that a mesh axis runs over, the one named last changes fastest.
Arguments:
- codes: bfloat16 [64, 256, 1024], P(('groups', 'blocks'), None, 'dims'), parts along dimension 0, may hold values from -6 to 6
- scales: bfloat16 [64, 256], P(('groups', 'blocks')), parts along dimension 0, may hold values from 0.5 to 2
- cluster_ids: int32 [64], P(('groups', 'blocks')), parts along dimension 0, may hold values from 0 to 2
- row_counts: int32 [64], P(('groups', 'blocks')), parts along dimension 0, may hold values from 64 to 256, as said below
- route_offsets: int32 [8, 2, 12, 1], P(('groups', 'blocks'), 'pairs'), parts along dimension 0, may hold values from 0 to 2; in each aligned block of 12 rows (0 to 11, 12 to 23, ..., all dimensions but the last counted through in order) at most 4 rows name the same one
- partner_local: int32 [8, 2, 12], P(('groups', 'blocks'), 'pairs'), parts along dimension 0, may hold values from 0 to 7
Outputs:
- log_density: float32 [64, 256], P(('groups', 'blocks')), parts along dimension 0
The draws below stay inside these ranges and needn't reach their ends.
There are 2 independent parts, one for each index of `groups`. The reference program is written for one: setup_inputs(seed, part) draws one part's arguments, and reference() takes and returns one part's arrays. A program takes and returns all parts, laid end to end along the dimension named above; each array names one. Nothing has to cross between parts.
Inputs may be any that keep to these rules, and one draw needn't show every extreme that they name: `route_offsets`: in the list of one index of blocks and pairs (12 entries) no offset appears more than 4 times, and some offset appears exactly 4 times. `row_counts`: in every draw some block uses all 256 rows.
All inputs are finite; a program needn't handle non-finite values.
Results may differ from the reference program's by a relative error of at most 0.0005.
Values may be sent and summed in bfloat16 or wider, within the bound.
No kernel may reach another device: no remote copies, remote signals or barrier semaphores. Data moves between devices by JAX's collectives and lax.ppermute only.
A program may use at most 64 MiB of HBM per device.

```python
import math
import jax
import jax.numpy as jnp
import numpy as np
from jax import lax

E = 1024
R = 256
BPD = 8
NCLUST = 3
PAIRS_DEV = 12
CAP = 4
NBLK = 32
N_BLOCKS = 4
N_PAIRS = 2


def draw_row_counts(key, part):
    key = jax.random.fold_in(key, 7)
    first_key, second_key = jax.random.split(key)
    counts = jax.random.randint(first_key, (NBLK,), R // 4, R + 1)
    full_block = jax.random.randint(second_key, (), 0, NBLK)
    return jnp.where(jnp.arange(NBLK) == full_block, R, counts).astype(jnp.int32)


def plant(array, own_key, low, high):
    shape = array.shape
    index_at = [jax.random.randint(jax.random.fold_in(own_key, axis), (), 0, shape[axis]) for axis in range(len(shape))]
    array = array.at[tuple(index_at)].set(low)
    longest = shape.index(max(shape))
    index_at[longest] = (index_at[longest] + 1) % shape[longest]
    return array.at[tuple(index_at)].set(high)


def levels(stream_key, dims, shards, smallest, high):
    loudness, own = 1.0, jax.random.fold_in(stream_key, 6)
    for position, shards_of in shards:
        steps = jnp.exp(jax.random.uniform(jax.random.fold_in(own, position), (shards_of,), jnp.float32, smallest / len(shards), high / len(shards)))
        loudness = loudness * jnp.repeat(steps, dims[position] // shards_of).reshape([-1 if axis == position else 1 for axis in range(len(dims))])
    return loudness


def deal_out(rng, own, number, rows, amount, top, reach, lean):
    ranking = jax.random.permutation(rng, amount)
    packed, usual = load_shares(amount, rows * top, reach, lean, True), load_shares(amount, rows * top, reach, lean, False)
    places = jnp.arange(amount)

    def named(lengths, rotation):
        used = int((lengths > 0).sum())
        fixed = max(1, used // 4)
        passed = fixed + (places - fixed + rotation * (used - fixed)) % max(1, amount - fixed)
        return jnp.zeros((amount,), jnp.int32).at[ranking[jnp.where(places < fixed, places, passed)]].set(jnp.asarray(lengths, jnp.int32))

    lengths = jnp.where(number % 4 == 0, named(packed, number // 4), named(usual, number - number // 4 - 1))
    mixed = jax.random.permutation(jax.random.fold_in(own, 3), amount)
    source_of, taker = mixed[0:amount // 2 * 2:2], mixed[1:amount // 2 * 2:2]
    room = jnp.minimum(lengths[source_of] - 1, reach - lengths[taker]) // 2
    room = jnp.where((source_of == ranking[0]) | (taker == ranking[0]) | (lengths[taker] == 0), 0, jnp.maximum(room, 0))
    passed = jax.random.randint(jax.random.fold_in(own, 4), (amount // 2,), 0, 1 << 20) % (room + 1)
    lengths = lengths.at[source_of].add(-passed).at[taker].add(passed)
    members = jnp.searchsorted(jnp.cumsum(lengths), jnp.arange(rows * top), side="right").astype(jnp.int32)
    listing = members.reshape(top, rows).T
    listing = listing[jax.random.permutation(jax.random.fold_in(own, 1), rows)]
    rotation = jax.random.randint(jax.random.fold_in(own, 2), (rows, 1), 0, top)
    return jnp.take_along_axis(listing, (jnp.arange(top)[None, :] + rotation) % top, axis=1)


def load_shares(amount, total, bound, skew, full):
    weights = [(1 << 20) // math.isqrt(grade ** skew) + 1 for grade in range(1, amount + 1)]
    largest = bound if full else min(bound, max(-(-total // amount), total * weights[0] // sum(weights)))
    least = 1 if total - largest >= amount - 1 else 0
    given, rest = [largest] + [least] * (amount - 1), total - largest - least * (amount - 1)
    while rest > 0:
        free = [i for i in range(1, amount) if given[i] < largest] or [i for i in range(1, amount) if given[i] < bound]
        whole, remaining = sum([weights[i] for i in free]), rest
        for i in free:
            more = min(bound - given[i], max(1, remaining * weights[i] // whole), rest)
            given[i] = given[i] + more
            rest = rest - more
    return np.array(given)


def noise(stream_key, dims, deviation, reach, cuts=(), kind=jnp.bfloat16):
    result = jax.random.normal(stream_key, dims, jnp.float32) * deviation
    if len(cuts) > 0:
        result = levels(stream_key, dims, cuts, -0.22, 0.18) * result
    return jnp.clip(result, min=-reach, max=reach).astype(kind)


def setup_inputs(seed: int = 0, part: int = 0) -> dict:
    seeds = jax.random.split(jax.random.key(seed), 7)
    own_keys = jax.random.split(jax.random.fold_in(seeds[6], part), 7)
    codes = noise(own_keys[0], (NBLK, R, E), 1.0, 6.0, ((0, 4), (2, 2)))
    scales = jnp.clip(jnp.exp(math.log(2.0) - 1.3862944 * jax.random.uniform(own_keys[1], (NBLK, R), jnp.float32) ** levels(own_keys[1], (NBLK, R), ((0, 4),), -0.2, 0.2)), 0.5, 2.0).astype(jnp.bfloat16)
    cluster_ids = plant(jax.random.randint(own_keys[2], (NBLK,), 0, NCLUST), jax.random.fold_in(own_keys[2], 1), 0, NCLUST - 1).astype(jnp.int32)
    row_counts = draw_row_counts(jax.random.fold_in(jax.random.fold_in(seeds[6], part), 71), part)
    route_offsets_keys = jax.random.split(jax.random.fold_in(own_keys[4], 1), N_BLOCKS * N_PAIRS * PAIRS_DEV // PAIRS_DEV)
    route_offsets_turns = jax.random.permutation(jax.random.fold_in(own_keys[4], 3), N_BLOCKS * N_PAIRS * PAIRS_DEV // PAIRS_DEV)
    route_offsets = jax.vmap(lambda own, number: deal_out(jax.random.fold_in(own_keys[4], 2), own, number, PAIRS_DEV, N_BLOCKS - 1, 1, CAP, 2))(route_offsets_keys, route_offsets_turns).reshape((N_BLOCKS, N_PAIRS, PAIRS_DEV, 1))
    partner_local = plant(jax.random.randint(own_keys[5], (N_BLOCKS, N_PAIRS, PAIRS_DEV), 0, BPD), jax.random.fold_in(own_keys[5], 1), 0, BPD - 1).astype(jnp.int32)
    return dict(codes=codes, scales=scales, cluster_ids=cluster_ids, row_counts=row_counts, route_offsets=route_offsets, partner_local=partner_local)


def reference(codes, scales, cluster_ids, row_counts, route_offsets, partner_local):
    highest = lax.Precision.HIGHEST
    inverse_root = 1.0 / math.sqrt(E)
    owner_ids = jnp.arange(N_BLOCKS, dtype=jnp.int32)
    target_owner = (owner_ids[:, None, None] + 1 + route_offsets[..., 0]) % N_BLOCKS
    partner_ids = (target_owner * BPD + partner_local).reshape(N_BLOCKS * N_PAIRS, PAIRS_DEV).astype(jnp.int32)
    requester_ids = jnp.repeat(owner_ids, N_PAIRS)
    valid_rows = (jnp.arange(R, dtype=jnp.int32)[None, :] < row_counts[:, None]).astype(jnp.float32)
    codes_wide = codes.astype(jnp.float32)
    scale_wide = scales.astype(jnp.float32)

    def requester_step(density, request):
        owner_index, partners = request
        first_block = (owner_index * BPD).astype(jnp.int32)
        local_codes = lax.dynamic_slice_in_dim(codes_wide, first_block, BPD, 0).reshape(BPD * R, E)
        local_scale = lax.dynamic_slice_in_dim(scale_wide, first_block, BPD, 0).reshape(BPD * R)
        local_valid = lax.dynamic_slice_in_dim(valid_rows, first_block, BPD, 0).reshape(BPD * R)
        local_cluster = jnp.repeat(lax.dynamic_slice_in_dim(cluster_ids, first_block, BPD, 0), R)
        partner_codes = codes_wide[partners]
        partner_scale = scale_wide[partners]
        partner_valid = valid_rows[partners]
        partner_cluster = cluster_ids[partners]
        gram_tile = jnp.einsum('ae,pre->apr', local_codes, partner_codes, precision=highest)
        kernel_tile = jnp.exp(gram_tile * (local_scale[:, None, None] * partner_scale[None, :, :]) * inverse_root)
        matches = (local_cluster[:, None] == partner_cluster[None, :]).astype(jnp.float32)
        kernel_tile = kernel_tile * (matches * local_valid[:, None])[:, :, None] * partner_valid[None, :, :]
        row_sums = lax.optimization_barrier(jnp.sum(kernel_tile, axis=(1, 2))).reshape(BPD, R)
        column_sums = lax.optimization_barrier(jnp.sum(kernel_tile, axis=0))
        current = lax.dynamic_slice_in_dim(density, first_block, BPD, 0)
        density = lax.dynamic_update_slice_in_dim(density, current + row_sums, first_block, 0)
        density = density.at[partners].add(column_sums)
        return (density, None)
    start_density = jnp.zeros((NBLK, R), jnp.float32)
    density, unused = lax.scan(requester_step, start_density, (requester_ids, partner_ids))
    return jnp.log1p(density)
```

```python
import functools
import math

import jax
import jax.numpy as jnp
from jax import lax
from jax.experimental import pallas as pl
from jax.experimental.pallas import tpu as pltpu
from jax.sharding import PartitionSpec as P

NT = (((1,), (1,)), ((), ()))


def tile_kernel(
    weight_ref, count_ref, own_ref, peer_ref, part_own_ref, part_peer_ref, scale_ref, part_scale_ref,
    rows_ref, columns_ref, total_ref,
):
    blocks, rows, _ = own_ref.shape
    part = part_own_ref.shape[0]
    lanes = 128
    rows_ref[...] = jnp.zeros_like(rows_ref)
    total_ref[...] = jnp.zeros_like(total_ref)
    part_rows = count_ref[blocks]
    part_valid = (lax.broadcasted_iota(jnp.int32, (part, 1), 0) < part_rows).astype(jnp.float32)
    part_scale = jnp.transpose(jnp.broadcast_to(part_scale_ref[...], (8, part)))[:, 0:1]
    for block in range(blocks):

        @pl.when(weight_ref[block] != 0.0)
        def _(block=block):
            gram = lax.dot_general(
                part_own_ref[...], own_ref[block], NT, preferred_element_type=jnp.float32
            ) + lax.dot_general(
                part_peer_ref[...], peer_ref[block], NT, preferred_element_type=jnp.float32
            )
            weight = weight_ref[block]
            row_valid = lax.broadcasted_iota(jnp.int32, (1, rows), 1) < count_ref[block]
            kern = jnp.exp(gram * (part_scale * scale_ref[block : block + 1, :]))
            kern = jnp.where(row_valid, kern, 0.0) * part_valid
            rows_ref[block : block + 1, :] = weight * jnp.sum(kern, axis=0, keepdims=True)
            folded = kern[:, 0:lanes]
            for start in range(lanes, rows, lanes):
                folded = folded + kern[:, start : start + lanes]
            total_ref[...] += weight * folded

    columns_ref[...] = jnp.sum(jnp.transpose(total_ref[...]), axis=0, keepdims=True)


def tile_sums(weights, counts, own, peer, part_own, part_peer, scale, part_scale):
    blocks, rows, width = own.shape
    part = part_own.shape[0]
    smem = pl.BlockSpec(memory_space=pltpu.SMEM)
    vmem = pl.BlockSpec(memory_space=pltpu.VMEM)
    return pl.pallas_call(
        tile_kernel,
        out_shape=(
            jax.ShapeDtypeStruct((blocks, rows), jnp.float32),
            jax.ShapeDtypeStruct((1, part), jnp.float32),
        ),
        in_specs=[smem, smem, vmem, vmem, vmem, vmem, vmem, vmem],
        out_specs=(vmem, vmem),
        scratch_shapes=[pltpu.VMEM((part, 128), jnp.float32)],
        compiler_params=pltpu.CompilerParams(vmem_limit_bytes=24 * 1024 * 1024),
        cost_estimate=pl.CostEstimate(
            flops=4 * blocks * rows * part * width,
            bytes_accessed=4 * blocks * rows * width + 4 * part * width,
            transcendentals=blocks * rows * part,
        ),
    )(weights, counts, own, peer, part_own, part_peer, scale, part_scale)


def per_device(codes, scales, cluster_ids, row_counts, route_offsets, partner_local):
    owners = lax.axis_size("blocks")
    pairs = lax.axis_size("pairs")
    owner = lax.axis_index("blocks")
    pair = lax.axis_index("pairs")
    core = lax.axis_index("dims")
    own_blocks, rows, width = codes.shape
    inverse_root = 1.0 / math.sqrt(width * lax.axis_size("dims"))
    total_rows = own_blocks * rows
    share = total_rows // pairs
    quarter = share // 4
    rounds = owners // 2
    swap = [(0, 1), (1, 0)]
    share_start = pair * share

    flat = codes.reshape(total_rows, width)
    first = lax.dynamic_slice_in_dim(flat, share_start, 2 * quarter, 0)
    peer_codes = lax.ppermute(codes, "dims", swap)
    second_start = share_start + (2 + core) * quarter
    second = jnp.stack([
        lax.dynamic_slice_in_dim(flat, second_start, quarter, 0),
        lax.dynamic_slice_in_dim(peer_codes.reshape(total_rows, width), second_start, quarter, 0),
    ])

    targets = (owner + 1 + route_offsets.reshape(-1)) % owners
    named = targets * own_blocks + partner_local.reshape(-1)
    block_ids = jnp.arange(owners * own_blocks, dtype=jnp.int32)
    counted = jnp.sum((named[None, :] == block_ids[:, None]).astype(jnp.float32), axis=1)
    listed = counted
    for step in range(1, pairs):
        listed = listed + lax.ppermute(
            counted, "pairs", [(i, (i + step) % pairs) for i in range(pairs)]
        )
    listed = listed.reshape(owners, own_blocks)

    scale_wide = scales.astype(jnp.float32)
    scale_root = scale_wide * inverse_root
    own_valid = row_counts

    def sends(step):
        if 2 * step == owners:
            return [((o + step - 1) % owners, (o + step) % owners) for o in range(owners // 2)]
        return [(i, (i + 1) % owners) for i in range(owners)]

    def origins(step):
        return owners // 2 if 2 * step == owners else owners

    row_total = jnp.zeros((own_blocks, rows), jnp.float32)
    column_total = jnp.zeros((total_rows,), jnp.float32)
    first_place = share_start + core * quarter
    for step in range(1, rounds + 1):
        perm = sends(step)
        direct = [(o, (o + step) % owners) for o in range(origins(step))]
        back = [(b, a) for a, b in direct]
        first = lax.ppermute(first, "blocks", perm)
        second = lax.ppermute(second, "blocks", perm)
        to_owner = (owner + step) % owners
        note = jnp.concatenate([
            cluster_ids.astype(jnp.float32),
            row_counts.astype(jnp.float32),
            lax.dynamic_index_in_dim(listed, to_owner, 0, keepdims=False),
        ])
        packed = jnp.concatenate([scale_wide.reshape(-1), note])
        packed = lax.ppermute(packed, "blocks", direct)
        from_owner = (owner - step) % owners
        active = (from_owner < origins(step)).astype(jnp.float32)
        part_scales = packed[:total_rows]
        part_cluster, part_counts, part_listed = [
            packed[total_rows + i * own_blocks : total_rows + (i + 1) * own_blocks] for i in range(3)
        ]
        own_listed = lax.dynamic_index_in_dim(listed, from_owner, 0, keepdims=False)
        all_weights = jnp.where(
            part_cluster[:, None] == cluster_ids.astype(jnp.float32)[None, :],
            own_listed[:, None] + part_listed[None, :],
            0.0,
        ) * active

        def chunk_sums(place, part_own, part_peer):
            block = place // rows
            offset = place % rows
            weights = lax.dynamic_index_in_dim(all_weights, block, 0, keepdims=False)
            left = lax.dynamic_index_in_dim(part_counts, block, 0).astype(jnp.int32) - offset
            counts = jnp.concatenate([row_counts, left])
            part_scale = lax.dynamic_slice_in_dim(part_scales, place, quarter, 0)[None, :]
            return tile_sums(
                weights, counts, codes, peer_codes, part_own, part_peer, scale_root, part_scale
            )

        mine = lax.dynamic_slice_in_dim(first, core * quarter, quarter, 0)
        other = lax.dynamic_slice_in_dim(first, (1 - core) * quarter, quarter, 0)
        first_rows, first_columns = chunk_sums(first_place, mine, lax.ppermute(other, "dims", swap))
        second_rows, second_columns = chunk_sums(second_start, second[0], second[1])
        row_total = row_total + first_rows + second_rows
        columns = lax.ppermute(
            jnp.concatenate([first_columns, second_columns], axis=0), "blocks", back
        )
        column_total = lax.dynamic_update_slice_in_dim(
            column_total,
            lax.dynamic_slice_in_dim(column_total, first_place, quarter, 0) + columns[0],
            first_place, 0,
        )
        column_total = lax.dynamic_update_slice_in_dim(
            column_total,
            lax.dynamic_slice_in_dim(column_total, second_start, quarter, 0) + columns[1],
            second_start, 0,
        )
    density = row_total + column_total.reshape(own_blocks, rows)
    density = lax.psum(density, ("pairs", "dims"))
    return jnp.log1p(density)


def solution(mesh):
    return jax.shard_map(
        per_device,
        mesh=mesh,
        in_specs=(
            P(("groups", "blocks"), None, "dims"),
            P(("groups", "blocks"), None),
            P(("groups", "blocks")),
            P(("groups", "blocks")),
            P(("groups", "blocks"), "pairs", None, None),
            P(("groups", "blocks"), "pairs", None),
        ),
        out_specs=P(("groups", "blocks"), None),
        check_vma=False,
    )
```

```python
import math

import jax
import jax.numpy as jnp
from jax import lax
from jax.experimental import pallas as pl
from jax.experimental.pallas import tpu as pltpu
from jax.sharding import PartitionSpec as P

NT = (((1,), (1,)), ((), ()))
LANES = 128


def tile_kernel(info_ref, units_ref, own_ref, peer_ref, *refs):
    count = len(refs) - 7
    parts = refs[:count]
    scale_ref, part_scale_ref, rows_ref, columns_ref, held_ref, total_ref, copied = refs[count:]
    blocks, rows, _ = own_ref.shape
    segments, unit = columns_ref.shape

    def part(half, segment):
        return parts[2 * segment + half][:unit, :]

    def copies(block):
        return [
            pltpu.make_async_copy(whole.at[block], held_ref.at[block, half], copied.at[block, half])
            for half, whole in enumerate((own_ref, peer_ref))
        ]

    valid, weights = [], []
    for segment in range(segments):
        first_row = units_ref[segment] * unit
        part_block = first_row // rows
        left = info_ref[4 * blocks + part_block] - (first_row - part_block * rows)
        valid.append(left)
        weights.append([
            jnp.where(
                (info_ref[3 * blocks + part_block] == info_ref[block]) & (left > 0),
                info_ref[2 * blocks + part_block] + info_ref[5 * blocks + block],
                0,
            ) * info_ref[6 * blocks]
            for block in range(blocks)
        ])
    needed = [sum(weights[segment][block] for segment in range(segments)) for block in range(blocks)]
    for block in range(blocks):

        @pl.when(needed[block] != 0)
        def _(block=block):
            for copy in copies(block):
                copy.start()

    rows_ref[...] = jnp.zeros_like(rows_ref)
    total_ref[...] = jnp.zeros_like(total_ref)
    for block in range(blocks):

        @pl.when(needed[block] != 0)
        def _(block=block):
            for copy in copies(block):
                copy.wait()
            for segment in range(segments):

                @pl.when(weights[segment][block] != 0)
                def _(segment=segment):
                    gram = lax.dot_general(
                        part(0, segment), held_ref[block, 0], NT, preferred_element_type=jnp.float32
                    ) + lax.dot_general(
                        part(1, segment), held_ref[block, 1], NT, preferred_element_type=jnp.float32
                    )
                    part_scale = jnp.transpose(jnp.broadcast_to(
                        part_scale_ref[pl.ds(units_ref[segment], 1), :], (8, unit)
                    ))[:, 0:1]
                    kern = jnp.exp(gram * (part_scale * scale_ref[block : block + 1, :]))
                    row_valid = lax.broadcasted_iota(jnp.int32, (1, rows), 1) < info_ref[blocks + block]
                    part_valid = lax.broadcasted_iota(jnp.int32, (unit, 1), 0) < valid[segment]
                    kern = jnp.where(row_valid & part_valid, kern, 0.0)
                    factor = weights[segment][block].astype(jnp.float32)
                    rows_ref[block : block + 1, :] += factor * jnp.sum(kern, axis=0, keepdims=True)
                    folded = kern[:, 0:LANES]
                    for start in range(LANES, rows, LANES):
                        folded = folded + kern[:, start : start + LANES]
                    total_ref[segment] += factor * folded

    for segment in range(segments):
        columns_ref[segment : segment + 1, :] = jnp.sum(
            jnp.transpose(total_ref[segment]), axis=0, keepdims=True
        )


def tile_sums(info, units, own, peer, parts, scale, part_scale):
    blocks, rows, width = own.shape
    segments, unit = len(parts) // 2, part_scale.shape[1]
    smem = pl.BlockSpec(memory_space=pltpu.SMEM)
    vmem = pl.BlockSpec(memory_space=pltpu.VMEM)
    held = pl.BlockSpec(memory_space=pl.ANY)
    return pl.pallas_call(
        tile_kernel,
        out_shape=(
            jax.ShapeDtypeStruct((blocks, rows), jnp.float32),
            jax.ShapeDtypeStruct((segments, unit), jnp.float32),
        ),
        in_specs=[smem, smem, held, held] + [vmem] * (2 + len(parts)),
        out_specs=(vmem, vmem),
        scratch_shapes=[
            pltpu.VMEM((blocks, 2, rows, width), own.dtype),
            pltpu.VMEM((segments, unit, LANES), jnp.float32),
            pltpu.SemaphoreType.DMA((blocks, 2)),
        ],
        compiler_params=pltpu.CompilerParams(vmem_limit_bytes=32 * 1024 * 1024),
        cost_estimate=pl.CostEstimate(flops=0, bytes_accessed=0, transcendentals=0),
    )(info, units, own, peer, *parts, scale, part_scale)


def per_device(codes, scales, cluster_ids, row_counts, route_offsets, partner_local):
    groups = lax.axis_size("groups")
    owners = lax.axis_size("blocks")
    pairs = lax.axis_size("pairs")
    group = lax.axis_index("groups")
    owner = lax.axis_index("blocks")
    pair = lax.axis_index("pairs")
    core = lax.axis_index("dims")
    blocks, rows, width = codes.shape
    inverse_root = 1.0 / math.sqrt(width * lax.axis_size("dims"))
    share = blocks * rows // pairs
    unit = share // 4
    rounds = owners // 2
    swap = [(0, 1), (1, 0)]
    line = ("groups", "blocks")

    def place(g, o):
        o = o % owners
        return g * owners + (o if g % 2 == 0 else owners - 1 - o)

    sign = jnp.where(group % 2 == 0, 1, -1)
    ring_place = jnp.where(group % 2 == 0, owner, owners - 1 - owner)

    def origins(step):
        return owners // 2 if 2 * step == owners else owners

    def moves(step, start, stop):
        return [
            (place(g, o + start), place(g, o + stop))
            for g in range(groups) for o in range(origins(step))
        ]

    def beside(at):
        return at + owners if at // owners % 2 == 0 else at - owners

    after = lax.optimization_barrier
    detour = groups % 2 == 0

    flat = codes.reshape(-1, width)

    def quarter(number):
        return lax.dynamic_slice_in_dim(flat, pair * share + number * unit, unit, 0)

    first = [quarter(1 - core)]
    first[0], flat, route_offsets, codes_held = after((first[0], flat, route_offsets, codes))
    first.append(quarter(core))
    second = [quarter(3 - core), quarter(2 + core)]

    def send(arrays, to):
        return [lax.ppermute(array, line, to) for array in arrays]

    first = send(first, moves(1, 0, 1))
    peer_codes = lax.ppermute(codes_held, "dims", swap)

    targets = (owner + 1 + route_offsets.reshape(-1)) % owners
    named = targets * blocks + partner_local.reshape(-1)
    block_ids = jnp.arange(owners * blocks, dtype=jnp.int32)
    counted = jnp.sum((named[None, :] == block_ids[:, None]).astype(jnp.float32), axis=1)
    listed = counted
    for step in range(1, pairs):
        listed = listed + lax.ppermute(
            counted, "pairs", [(i, (i + step) % pairs) for i in range(pairs)]
        )
    note = jnp.concatenate([
        value.reshape(-1).astype(codes.dtype) for value in (scales, cluster_ids, row_counts, listed)
    ])
    note_rows = -(-note.shape[0] // (16 * width)) * 16
    note = jnp.pad(note, (0, note_rows * width - note.shape[0])).reshape(note_rows, width)
    own_listed = listed.reshape(owners, blocks).astype(jnp.int32)
    second[0] = jnp.concatenate([second[0], note], axis=0)
    second[0], second[1] = after((second[0], second[1]))
    second = send(second, moves(1, 0, 1))

    scale_root = scales.astype(jnp.float32) * inverse_root
    units = jnp.stack([pair * 4 + core, pair * 4 + core + 2]).astype(jnp.int32)

    row_parts, column_parts = [], []
    for step in range(1, rounds + 1):
        held, held_second = list(first), list(second)
        if step < rounds:
            perm = moves(step + 1, step, step + 1)
            if detour:
                aside = [(s, beside(s)) for s, _ in perm]
                home = [(beside(s), t) for s, t in perm]
                one = lax.ppermute(held[0], line, aside)
                one, held[1] = after((one, held[1]))
                two = lax.ppermute(held[1], line, aside)
                two, held_second[0] = after((two, held_second[0]))
                held_second[0], held_second[1] = after((held_second[0], held_second[1]))
                first = send([one, two], home)
            else:
                first = send(held, perm)
            second = send(held_second, perm)
        note = held_second[0][unit:].reshape(-1)
        scale_end = blocks * rows
        cluster_end, count_end = scale_end + blocks, scale_end + 2 * blocks
        part_scale = note[:scale_end].astype(jnp.float32).reshape(-1, unit)
        from_owner = (owner - sign * step) % owners
        active = ((ring_place - step) % owners) < origins(step)
        info = jnp.concatenate([
            cluster_ids,
            row_counts,
            lax.dynamic_index_in_dim(own_listed, from_owner, 0, keepdims=False),
            note[scale_end:count_end].astype(jnp.int32),
            lax.dynamic_slice_in_dim(note, count_end + owner * blocks, blocks, 0).astype(jnp.int32),
            active.astype(jnp.int32)[None],
        ])
        others = [lax.ppermute(part, "dims", swap) for part in (held[0], held_second[0])]
        row_sums, columns = tile_sums(
            info, units, codes, peer_codes, [held[1], others[0], held_second[1], others[1]],
            scale_root, part_scale,
        )
        row_parts.append(row_sums)
        columns = lax.ppermute(
            columns, line,
            [(place(g, o + step), place(g, o)) for g in range(groups) for o in range(owners)],
        )
        column_parts.append(columns)
        if step < rounds:
            first[0], first[1], second[0], second[1], columns = after(
                (first[0], first[1], second[0], second[1], columns)
            )
    here = (jnp.arange(pairs)[:, None] == pair) & (jnp.arange(2)[None, :] == core)
    column_total = jnp.where(here[:, None, :, None], sum(column_parts)[None, :, None, :], 0.0)
    density = sum(row_parts) + column_total.reshape(blocks, rows)
    density = lax.psum(density, ("pairs", "dims"))
    return jnp.log1p(density)


def solution(mesh):
    return jax.shard_map(
        per_device,
        mesh=mesh,
        in_specs=(
            P(("groups", "blocks"), None, "dims"),
            P(("groups", "blocks"), None),
            P(("groups", "blocks")),
            P(("groups", "blocks")),
            P(("groups", "blocks"), "pairs", None, None),
            P(("groups", "blocks"), "pairs", None),
        ),
        out_specs=P(("groups", "blocks"), None),
        check_vma=False,
    )
```

```python
import math

import jax
import jax.numpy as jnp
from jax import lax
from jax.experimental import pallas as pl
from jax.experimental.pallas import tpu as pltpu
from jax.sharding import PartitionSpec as P

NT = (((1,), (1,)), ((), ()))
LANES = 128


def tile_kernel(info_ref, units_ref, own_ref, peer_ref, *refs):
    count = len(refs) - 7
    parts = refs[:count]
    scale_ref, part_scale_ref, rows_ref, columns_ref, held_ref, total_ref, copied = refs[count:]
    blocks, rows, _ = own_ref.shape
    segments, unit = columns_ref.shape

    def part(half, segment):
        return parts[2 * segment + half][:unit, :]

    def copies(block):
        return [
            pltpu.make_async_copy(whole.at[block], held_ref.at[block, half], copied.at[block, half])
            for half, whole in enumerate((own_ref, peer_ref))
        ]

    valid, weights = [], []
    for segment in range(segments):
        first_row = units_ref[segment] * unit
        part_block = first_row // rows
        left = info_ref[4 * blocks + part_block] - (first_row - part_block * rows)
        valid.append(left)
        weights.append([
            jnp.where(
                (info_ref[3 * blocks + part_block] == info_ref[block]) & (left > 0),
                info_ref[2 * blocks + part_block] + info_ref[5 * blocks + block],
                0,
            ) * info_ref[6 * blocks]
            for block in range(blocks)
        ])
    needed = [sum(weights[segment][block] for segment in range(segments)) for block in range(blocks)]
    for block in range(blocks):

        @pl.when(needed[block] != 0)
        def _(block=block):
            for copy in copies(block):
                copy.start()

    rows_ref[...] = jnp.zeros_like(rows_ref)
    total_ref[...] = jnp.zeros_like(total_ref)
    for block in range(blocks):

        @pl.when(needed[block] != 0)
        def _(block=block):
            for copy in copies(block):
                copy.wait()
            for segment in range(segments):

                @pl.when(weights[segment][block] != 0)
                def _(segment=segment):
                    gram = lax.dot_general(
                        part(0, segment), held_ref[block, 0], NT, preferred_element_type=jnp.float32
                    ) + lax.dot_general(
                        part(1, segment), held_ref[block, 1], NT, preferred_element_type=jnp.float32
                    )
                    part_scale = jnp.transpose(jnp.broadcast_to(
                        part_scale_ref[pl.ds(units_ref[segment], 1), :], (8, unit)
                    ))[:, 0:1]
                    kern = jnp.exp(gram * (part_scale * scale_ref[block : block + 1, :]))
                    row_valid = lax.broadcasted_iota(jnp.int32, (1, rows), 1) < info_ref[blocks + block]
                    part_valid = lax.broadcasted_iota(jnp.int32, (unit, 1), 0) < valid[segment]
                    kern = jnp.where(row_valid & part_valid, kern, 0.0)
                    factor = weights[segment][block].astype(jnp.float32)
                    rows_ref[block : block + 1, :] += factor * jnp.sum(kern, axis=0, keepdims=True)
                    folded = kern[:, 0:LANES]
                    for start in range(LANES, rows, LANES):
                        folded = folded + kern[:, start : start + LANES]
                    total_ref[segment] += factor * folded

    for segment in range(segments):
        columns_ref[segment : segment + 1, :] = jnp.sum(
            jnp.transpose(total_ref[segment]), axis=0, keepdims=True
        )


def tile_sums(info, units, own, peer, parts, scale, part_scale):
    blocks, rows, width = own.shape
    segments, unit = len(parts) // 2, part_scale.shape[1]
    smem = pl.BlockSpec(memory_space=pltpu.SMEM)
    vmem = pl.BlockSpec(memory_space=pltpu.VMEM)
    held = pl.BlockSpec(memory_space=pl.ANY)
    return pl.pallas_call(
        tile_kernel,
        out_shape=(
            jax.ShapeDtypeStruct((blocks, rows), jnp.float32),
            jax.ShapeDtypeStruct((segments, unit), jnp.float32),
        ),
        in_specs=[smem, smem, held, held] + [vmem] * (2 + len(parts)),
        out_specs=(vmem, vmem),
        scratch_shapes=[
            pltpu.VMEM((blocks, 2, rows, width), own.dtype),
            pltpu.VMEM((segments, unit, LANES), jnp.float32),
            pltpu.SemaphoreType.DMA((blocks, 2)),
        ],
        compiler_params=pltpu.CompilerParams(vmem_limit_bytes=32 * 1024 * 1024),
        cost_estimate=pl.CostEstimate(flops=0, bytes_accessed=0, transcendentals=0),
    )(info, units, own, peer, *parts, scale, part_scale)


def per_device(codes, scales, cluster_ids, row_counts, route_offsets, partner_local):
    groups = lax.axis_size("groups")
    owners = lax.axis_size("blocks")
    pairs = lax.axis_size("pairs")
    group = lax.axis_index("groups")
    owner = lax.axis_index("blocks")
    pair = lax.axis_index("pairs")
    core = lax.axis_index("dims")
    blocks, rows, width = codes.shape
    inverse_root = 1.0 / math.sqrt(width * lax.axis_size("dims"))
    share = blocks * rows // pairs
    unit = share // 4
    rounds = owners // 2
    swap = [(0, 1), (1, 0)]
    line = ("groups", "blocks")

    def place(g, o):
        o = o % owners
        return g * owners + (o if g % 2 == 0 else owners - 1 - o)

    sign = jnp.where(group % 2 == 0, 1, -1)
    ring_place = jnp.where(group % 2 == 0, owner, owners - 1 - owner)

    def origins(step):
        return owners // 2 if 2 * step == owners else owners

    def moves(step, start, stop):
        return [
            (place(g, o + start), place(g, o + stop))
            for g in range(groups) for o in range(origins(step))
        ]

    def beside(at):
        return at + owners if at // owners % 2 == 0 else at - owners

    after = lax.optimization_barrier
    detour = groups % 2 == 0

    flat = codes.reshape(-1, width)

    def quarter(number):
        return lax.dynamic_slice_in_dim(flat, pair * share + number * unit, unit, 0)

    def follow(value, *others):
        return lax.optimization_barrier((value, *others))[0]

    def send(arrays, to):
        return [lax.ppermute(array, line, to) for array in arrays]

    first = [quarter(1 - core)]
    flat = follow(flat, first[0])
    first.append(quarter(core))
    second = [quarter(3 - core), quarter(2 + core)]
    peer_codes = lax.ppermute(follow(codes, first[0]), "dims", swap)
    route_offsets = follow(route_offsets, peer_codes)
    first = send(first, moves(1, 0, 1))

    targets = (owner + 1 + route_offsets.reshape(-1)) % owners
    named = targets * blocks + partner_local.reshape(-1)
    block_ids = jnp.arange(owners * blocks, dtype=jnp.int32)
    counted = jnp.sum((named[None, :] == block_ids[:, None]).astype(jnp.float32), axis=1)
    listed = counted
    for step in range(1, pairs):
        listed = listed + lax.ppermute(
            counted, "pairs", [(i, (i + step) % pairs) for i in range(pairs)]
        )
    note = jnp.concatenate([
        value.reshape(-1).astype(codes.dtype) for value in (scales, cluster_ids, row_counts, listed)
    ])
    note_rows = -(-note.shape[0] // (16 * width)) * 16
    note = jnp.pad(note, (0, note_rows * width - note.shape[0])).reshape(note_rows, width)
    own_listed = listed.reshape(owners, blocks).astype(jnp.int32)
    second[0] = jnp.concatenate([second[0], note], axis=0)
    ready = second[0]
    second[1] = follow(second[1], first[0])
    second = send(second, moves(1, 0, 1))

    scale_root = scales.astype(jnp.float32) * inverse_root
    units = jnp.stack([pair * 4 + core, pair * 4 + core + 2]).astype(jnp.int32)

    row_parts, column_parts = [], []
    given = None
    for step in range(1, rounds + 1):
        held, held_second = list(first), list(second)
        if step < rounds:
            perm = moves(step + 1, step, step + 1)
            if detour:
                aside = [(s, beside(s)) for s, _ in perm]
                home = [(beside(s), t) for s, t in perm]
                one = lax.ppermute(follow(held[0], ready), line, aside)
                two = lax.ppermute(held[1], line, aside)
                first = send([one, two], home)
                second = send([follow(held_second[0], one), held_second[1]], perm)
            else:
                first, second = send(held, perm), send(held_second, perm)
        note = held_second[0][unit:].reshape(-1)
        scale_end = blocks * rows
        cluster_end, count_end = scale_end + blocks, scale_end + 2 * blocks
        part_scale = note[:scale_end].astype(jnp.float32).reshape(-1, unit)
        from_owner = (owner - sign * step) % owners
        active = ((ring_place - step) % owners) < origins(step)
        info = jnp.concatenate([
            cluster_ids,
            row_counts,
            lax.dynamic_index_in_dim(own_listed, from_owner, 0, keepdims=False),
            note[scale_end:count_end].astype(jnp.int32),
            lax.dynamic_slice_in_dim(note, count_end + owner * blocks, blocks, 0).astype(jnp.int32),
            active.astype(jnp.int32)[None],
        ])
        others = given or [lax.ppermute(part, "dims", swap) for part in (held[0], held_second[0])]
        if step < rounds:
            given = [lax.ppermute(part, "dims", swap) for part in (first[0], second[0])]
            info = follow(info, first[0], second[0])
        row_sums, columns = tile_sums(
            info, units, codes, peer_codes,
            [held[1], others[0], follow(held_second[1], others[0], others[1], info), others[1]],
            scale_root, part_scale,
        )
        row_parts.append(row_sums)
        columns = lax.ppermute(
            columns, line,
            [(place(g, o + step), place(g, o)) for g in range(groups) for o in range(owners)],
        )
        column_parts.append(columns)
        if step < rounds:
            first[1], second[1] = follow(first[1], columns), follow(second[1], columns)
    here = (jnp.arange(pairs)[:, None] == pair) & (jnp.arange(2)[None, :] == core)
    column_total = jnp.where(here[:, None, :, None], sum(column_parts)[None, :, None, :], 0.0)
    density = sum(row_parts) + column_total.reshape(blocks, rows)
    density = lax.psum(density, ("pairs", "dims"))
    return jnp.log1p(density)


def solution(mesh):
    return jax.shard_map(
        per_device,
        mesh=mesh,
        in_specs=(
            P(("groups", "blocks"), None, "dims"),
            P(("groups", "blocks"), None),
            P(("groups", "blocks")),
            P(("groups", "blocks")),
            P(("groups", "blocks"), "pairs", None, None),
            P(("groups", "blocks"), "pairs", None),
        ),
        out_specs=P(("groups", "blocks"), None),
        check_vma=False,
    )
```

```python
import math

import jax
import jax.numpy as jnp
from jax import lax
from jax.experimental import pallas as pl
from jax.experimental.pallas import tpu as pltpu
from jax.sharding import PartitionSpec as P

NT = (((1,), (1,)), ((), ()))
LANES = 128
LOG2E = math.log2(math.e)


def tile_kernel(info_ref, units_ref, own_ref, peer_ref, *refs):
    count = len(refs) - 8
    parts = refs[:count]
    (scale_ref, part_scale_ref, rows_ref, columns_ref,
     held_ref, total_ref, wide_ref, copied) = refs[count:]
    blocks, rows, _ = own_ref.shape
    segments, unit = columns_ref.shape

    def part(half, segment):
        return parts[2 * segment + half][:unit, :]

    def copies(block):
        return [
            pltpu.make_async_copy(whole.at[block], held_ref.at[block, half], copied.at[block, half])
            for half, whole in enumerate((own_ref, peer_ref))
        ]

    valid, weights = [], []
    for segment in range(segments):
        first_row = units_ref[segment] * unit
        part_block = first_row // rows
        left = info_ref[4 * blocks + part_block] - (first_row - part_block * rows)
        valid.append(left)
        weights.append([
            jnp.where(
                (info_ref[3 * blocks + part_block] == info_ref[block]) & (left > 0),
                info_ref[2 * blocks + part_block] + info_ref[5 * blocks + block],
                0,
            ) * info_ref[6 * blocks]
            for block in range(blocks)
        ])
    needed = [sum(weights[segment][block] for segment in range(segments)) for block in range(blocks)]
    for block in range(blocks):

        @pl.when(needed[block] != 0)
        def _(block=block):
            for copy in copies(block):
                copy.start()

    for segment in range(segments):
        part_scale = jnp.broadcast_to(part_scale_ref[pl.ds(units_ref[segment], 1), :], (LANES, unit))
        wide_ref[0, segment] = jnp.transpose(part_scale)
        row_ids = lax.broadcasted_iota(jnp.int32, (unit, LANES), 0)
        wide_ref[1, segment] = (row_ids < valid[segment]).astype(jnp.float32)
    rows_ref[...] = jnp.zeros_like(rows_ref)
    total_ref[...] = jnp.zeros_like(total_ref)
    for block in range(blocks):

        @pl.when(needed[block] != 0)
        def _(block=block):
            for copy in copies(block):
                copy.wait()
            for segment in range(segments):

                @pl.when(weights[segment][block] != 0)
                def _(segment=segment):
                    gram = lax.dot_general(
                        part(0, segment), held_ref[block, 0], NT, preferred_element_type=jnp.float32
                    ) + lax.dot_general(
                        part(1, segment), held_ref[block, 1], NT, preferred_element_type=jnp.float32
                    )
                    factor = weights[segment][block].astype(jnp.float32)
                    row_ids = lax.broadcasted_iota(jnp.int32, (1, LANES), 1)
                    for start in range(0, rows, LANES):
                        own_scale = scale_ref[block : block + 1, start : start + LANES] * LOG2E
                        own_valid = jnp.where(
                            row_ids + start < info_ref[blocks + block], factor, 0.0
                        )
                        summed = jnp.zeros((8, LANES), jnp.float32)
                        for at in range(0, unit, 64):
                            scaled = gram[at : at + 64, start : start + LANES] * (
                                wide_ref[0, segment, at : at + 64, :] * own_scale
                            )
                            kern = jnp.exp2(scaled) * wide_ref[1, segment, at : at + 64, :]
                            summed = summed + jnp.sum(kern.reshape(-1, 8, LANES), axis=0)
                            total_ref[segment, at : at + 64, :] += kern * own_valid
                        rows_ref[block : block + 1, start : start + LANES] += own_valid * jnp.sum(
                            summed, axis=0, keepdims=True
                        )

    for segment in range(segments):
        columns_ref[segment : segment + 1, :] = jnp.sum(
            jnp.transpose(total_ref[segment]), axis=0, keepdims=True
        )


def tile_sums(info, units, own, peer, parts, scale, part_scale):
    blocks, rows, width = own.shape
    segments, unit = len(parts) // 2, part_scale.shape[1]
    smem = pl.BlockSpec(memory_space=pltpu.SMEM)
    vmem = pl.BlockSpec(memory_space=pltpu.VMEM)
    held = pl.BlockSpec(memory_space=pl.ANY)
    return pl.pallas_call(
        tile_kernel,
        out_shape=(
            jax.ShapeDtypeStruct((blocks, rows), jnp.float32),
            jax.ShapeDtypeStruct((segments, unit), jnp.float32),
        ),
        in_specs=[smem, smem, held, held] + [vmem] * (2 + len(parts)),
        out_specs=(vmem, vmem),
        scratch_shapes=[
            pltpu.VMEM((blocks, 2, rows, width), own.dtype),
            pltpu.VMEM((segments, unit, LANES), jnp.float32),
            pltpu.VMEM((2, segments, unit, LANES), jnp.float32),
            pltpu.SemaphoreType.DMA((blocks, 2)),
        ],
        compiler_params=pltpu.CompilerParams(vmem_limit_bytes=32 * 1024 * 1024),
        cost_estimate=pl.CostEstimate(flops=0, bytes_accessed=0, transcendentals=0),
    )(info, units, own, peer, *parts, scale, part_scale)


def per_device(codes, scales, cluster_ids, row_counts, route_offsets, partner_local):
    groups = lax.axis_size("groups")
    owners = lax.axis_size("blocks")
    pairs = lax.axis_size("pairs")
    group = lax.axis_index("groups")
    owner = lax.axis_index("blocks")
    pair = lax.axis_index("pairs")
    core = lax.axis_index("dims")
    blocks, rows, width = codes.shape
    inverse_root = 1.0 / math.sqrt(width * lax.axis_size("dims"))
    share = blocks * rows // pairs
    unit = share // 4
    rounds = owners // 2
    swap = [(0, 1), (1, 0)]
    line = ("groups", "blocks")

    def place(g, o):
        o = o % owners
        return g * owners + (o if g % 2 == 0 else owners - 1 - o)

    sign = jnp.where(group % 2 == 0, 1, -1)
    ring_place = jnp.where(group % 2 == 0, owner, owners - 1 - owner)

    def origins(step):
        return owners // 2 if 2 * step == owners else owners

    def moves(step, start, stop):
        return [
            (place(g, o + start), place(g, o + stop))
            for g in range(groups) for o in range(origins(step))
        ]

    def beside(at):
        return at + owners if at // owners % 2 == 0 else at - owners

    after = lax.optimization_barrier
    detour = groups % 2 == 0

    flat = codes.reshape(-1, width)

    def quarter(number):
        return lax.dynamic_slice_in_dim(flat, pair * share + number * unit, unit, 0)

    def follow(value, *others):
        return lax.optimization_barrier((value, *others))[0]

    def send(arrays, to):
        return [lax.ppermute(array, line, to) for array in arrays]

    first = [quarter(1 - core)]
    flat = follow(flat, first[0])
    first.append(quarter(core))
    second = [quarter(3 - core), quarter(2 + core)]
    peer_codes = lax.ppermute(codes, "dims", swap)
    sliced = first[0]
    first = send(first, moves(1, 0, 1))

    route_offsets = follow(route_offsets, peer_codes)
    targets = (owner + 1 + route_offsets.reshape(-1)) % owners
    named = targets * blocks + partner_local.reshape(-1)
    block_ids = jnp.arange(owners * blocks, dtype=jnp.int32)
    counted = jnp.sum((named[None, :] == block_ids[:, None]).astype(jnp.float32), axis=1)
    listed = counted
    for step in range(1, pairs):
        listed = listed + lax.ppermute(
            counted, "pairs", [(i, (i + step) % pairs) for i in range(pairs)]
        )
    note = jnp.concatenate([
        value.reshape(-1).astype(codes.dtype) for value in (scales, cluster_ids, row_counts, listed)
    ])
    note_rows = -(-note.shape[0] // (16 * width)) * 16
    note = jnp.pad(note, (0, note_rows * width - note.shape[0])).reshape(note_rows, width)
    own_listed = listed.reshape(owners, blocks).astype(jnp.int32)
    second[0] = jnp.concatenate([second[0], note], axis=0)
    ready = second[0]
    second[1] = follow(second[1], first[0])
    second = send(second, moves(1, 0, 1))

    scale_root = scales.astype(jnp.float32) * inverse_root
    units = jnp.stack([pair * 4 + core, pair * 4 + core + 2]).astype(jnp.int32)

    def exchanged(part):
        return lax.ppermute(part, "dims", swap)

    row_parts, column_parts = [], []
    others = [None, None]
    for step in range(1, rounds + 1):
        held, held_second = list(first), list(second)
        if step < rounds:
            perm = moves(step + 1, step, step + 1)
            if detour:
                aside = [(s, beside(s)) for s, _ in perm]
                home = [(beside(s), t) for s, t in perm]
                one = lax.ppermute(follow(held[0], ready), line, aside)
                two = lax.ppermute(held[1], line, aside)
                first = send([one, two], home)
            else:
                one, two = held
                first = send(held, perm)
            second[0] = lax.ppermute(follow(held_second[0], one), line, perm)
        note = held_second[0][unit:].reshape(-1)
        scale_end = blocks * rows
        cluster_end, count_end = scale_end + blocks, scale_end + 2 * blocks
        part_scale = note[:scale_end].astype(jnp.float32).reshape(-1, unit)
        from_owner = (owner - sign * step) % owners
        active = ((ring_place - step) % owners) < origins(step)
        info = jnp.concatenate([
            cluster_ids,
            row_counts,
            lax.dynamic_index_in_dim(own_listed, from_owner, 0, keepdims=False),
            note[scale_end:count_end].astype(jnp.int32),
            lax.dynamic_slice_in_dim(note, count_end + owner * blocks, blocks, 0).astype(jnp.int32),
            active.astype(jnp.int32)[None],
        ])
        if others[0] is None:
            others[0] = exchanged(held[0])
        if others[1] is None:
            others[1] = exchanged(held_second[0])
        chunks = [held[1], others[0], follow(held_second[1], others[0], others[1], info), others[1]]
        others = [None, None]
        if step < rounds:
            others[1] = exchanged(second[0])
            info = follow(info, one)
            second[1] = lax.ppermute(held_second[1], line, perm)
        row_sums, columns = tile_sums(
            info, units, codes, peer_codes, chunks, scale_root, part_scale
        )
        row_parts.append(row_sums)
        if step < rounds:
            columns = follow(columns, row_sums)
        if step < rounds or pairs != 2:
            columns = lax.ppermute(
                columns, line,
                [(place(g, o + step), place(g, o)) for g in range(groups) for o in range(owners)],
            )
            column_parts.append(columns)
        if step < rounds:
            first[0] = follow(first[0], row_sums)
            first[1], second[1] = follow(first[1], columns), follow(second[1], columns)
    cores = jnp.arange(2)[None, :] == core
    here = (jnp.arange(pairs)[:, None] == pair) & cores
    density = sum(row_parts)
    if column_parts:
        density = density + jnp.where(
            here[:, None, :, None], sum(column_parts)[None, :, None, :], 0.0
        ).reshape(blocks, rows)
    if pairs != 2:
        return jnp.log1p(lax.psum(density, ("pairs", "dims")))
    outgoing = jnp.where(cores[:, :, None], columns[:, None, :], 0.0).reshape(-1, rows)
    both = jnp.concatenate([density, outgoing], axis=0)
    both = both + lax.ppermute(both, "dims", swap)
    density, outgoing = both[:blocks], both[blocks:]
    across = [(0, 1), (1, 0)]
    joint = ("groups", "blocks", "pairs")
    back = [
        (place(g, o + rounds) * 2 + p, place(g, o) * 2, p)
        for g in range(groups) for o in range(owners) for p in range(2)
    ]
    parts = [
        lax.ppermute(density, "pairs", across),
        lax.ppermute(outgoing, joint, [(s, t + p) for s, t, p in back]),
        lax.ppermute(outgoing, joint, [(s, t + 1 - p) for s, t, p in back]),
    ]
    straight, crossed = parts[1].reshape(1, -1, rows), parts[2].reshape(1, -1, rows)
    own_pair = (jnp.arange(2) == pair)[:, None, None]
    columns = jnp.where(own_pair, straight, crossed).reshape(blocks, rows)
    return jnp.log1p(density + parts[0] + columns)


def solution(mesh):
    return jax.shard_map(
        per_device,
        mesh=mesh,
        in_specs=(
            P(("groups", "blocks"), None, "dims"),
            P(("groups", "blocks"), None),
            P(("groups", "blocks")),
            P(("groups", "blocks")),
            P(("groups", "blocks"), "pairs", None, None),
            P(("groups", "blocks"), "pairs", None),
        ),
        out_specs=P(("groups", "blocks"), None),
        check_vma=False,
    )
```

```python
import functools
import math

import jax
import jax.numpy as jnp
from jax import lax
from jax.experimental import pallas as pl
from jax.experimental.pallas import tpu as pltpu
from jax.sharding import PartitionSpec as P

NT = (((1,), (1,)), ((), ()))
LANES = 128
LOG2E = math.log2(math.e)


def tile_kernel(info_ref, units_ref, own_ref, peer_ref, *refs):
    count = len(refs) - 11
    parts = refs[:count]
    (scale_ref, rows_ref, columns_ref, held_ref, total_ref, wide_ref, part_ref, raw_ref, note_ref,
     copied, part_copied) = refs[count:]
    blocks, rows, width = own_ref.shape
    segments, unit = columns_ref.shape

    def copies(block):
        return [
            pltpu.make_async_copy(whole.at[block], held_ref.at[block, half], copied.at[block, half])
            for half, whole in enumerate((own_ref, peer_ref))
        ]

    note_rows = parts[-1].shape[0] - unit
    part_copies = [
        pltpu.make_async_copy(
            part.at[pl.ds(0, unit)], part_ref.at[i % 2, pl.ds(i // 2 * unit, unit)], part_copied.at[i]
        )
        for i, part in enumerate(parts)
    ]
    part_copies.append(pltpu.make_async_copy(
        parts[-1].at[pl.ds(unit, note_rows)], raw_ref, part_copied.at[count]
    ))
    for copy in part_copies:
        copy.start()
    valid, weights = [], []
    for segment in range(segments):
        first_row = units_ref[segment] * unit
        part_block = first_row // rows
        left = info_ref[4 * blocks + part_block] - (first_row - part_block * rows)
        valid.append(left)
        weights.append([
            jnp.where(
                (info_ref[3 * blocks + part_block] == info_ref[block]) & (left > 0),
                info_ref[2 * blocks + part_block] + info_ref[5 * blocks + block],
                0,
            ) * info_ref[6 * blocks]
            for block in range(blocks)
        ])
    needed = [sum(weights[segment][block] for segment in range(segments)) for block in range(blocks)]
    for block in range(blocks):

        @pl.when(needed[block] != 0)
        def _(block=block):
            for copy in copies(block):
                copy.start()

    rows_ref[...] = jnp.zeros_like(rows_ref)
    total_ref[...] = jnp.zeros_like(total_ref)
    for copy in part_copies:
        copy.wait()
    note_ref[...] = raw_ref[...].astype(jnp.float32)
    in_row = width // unit
    for segment in range(segments):
        line = note_ref[pl.ds(units_ref[segment] // in_row, 1), :]
        at = units_ref[segment] % in_row
        part_scale = line[:, :unit]
        for i in range(1, in_row):
            part_scale = jnp.where(at == i, line[:, i * unit : (i + 1) * unit], part_scale)
        wide_ref[0, segment] = jnp.transpose(jnp.broadcast_to(part_scale, (LANES, unit)))
        row_ids = lax.broadcasted_iota(jnp.int32, (unit, LANES), 0)
        wide_ref[1, segment] = (row_ids < valid[segment]).astype(jnp.float32)

    def product(block, first, length):
        return sum(
            lax.dot_general(
                part_ref[half, first : first + length, :], held_ref[block, half], NT,
                preferred_element_type=jnp.float32,
            )
            for half in range(2)
        )

    def tile(segment, block, gram):
        factor = weights[segment][block].astype(jnp.float32)
        row_ids = lax.broadcasted_iota(jnp.int32, (1, LANES), 1)
        for start in range(0, rows, LANES):
            own_scale = scale_ref[block : block + 1, start : start + LANES] * LOG2E
            own_valid = jnp.where(row_ids + start < info_ref[blocks + block], factor, 0.0)
            summed = jnp.zeros((8, LANES), jnp.float32)
            for at in range(0, unit, 64):
                here = pl.ds(at, 64)
                scaled = gram[at : at + 64, start : start + LANES] * (
                    wide_ref[0, segment, here, :] * own_scale
                )
                kern = jnp.exp2(scaled) * wide_ref[1, segment, here, :]
                summed = summed + jnp.sum(kern.reshape(-1, 8, LANES), axis=0)
                total_ref[segment, here, :] += kern * own_valid
            rows_ref[block : block + 1, start : start + LANES] += own_valid * jnp.sum(
                summed, axis=0, keepdims=True
            )

    for block in range(blocks):

        @pl.when(needed[block] != 0)
        def _(block=block):
            for copy in copies(block):
                copy.wait()
            wanted = [weights[segment][block] != 0 for segment in range(segments)]
            every = functools.reduce(jnp.logical_and, wanted)

            @pl.when(every)
            def _():
                gram = product(block, 0, segments * unit)
                for segment in range(segments):
                    tile(segment, block, gram[segment * unit : (segment + 1) * unit])

            for segment in range(segments):

                @pl.when(wanted[segment] & jnp.logical_not(every))
                def _(segment=segment):
                    tile(segment, block, product(block, segment * unit, unit))

    for segment in range(segments):
        columns_ref[segment : segment + 1, :] = jnp.sum(
            jnp.transpose(total_ref[segment]), axis=0, keepdims=True
        )


def tile_sums(info, units, own, peer, parts, scale):
    blocks, rows, width = own.shape
    segments, unit = len(parts) // 2, parts[0].shape[0]
    smem = pl.BlockSpec(memory_space=pltpu.SMEM)
    vmem = pl.BlockSpec(memory_space=pltpu.VMEM)
    held = pl.BlockSpec(memory_space=pl.ANY)
    return pl.pallas_call(
        tile_kernel,
        out_shape=(
            jax.ShapeDtypeStruct((blocks, rows), jnp.float32),
            jax.ShapeDtypeStruct((segments, unit), jnp.float32),
        ),
        in_specs=[smem, smem, held, held] + [held] * len(parts) + [vmem],
        out_specs=(vmem, vmem),
        scratch_shapes=[
            pltpu.VMEM((blocks, 2, rows, width), own.dtype),
            pltpu.VMEM((segments, unit, LANES), jnp.float32),
            pltpu.VMEM((2, segments, unit, LANES), jnp.float32),
            pltpu.VMEM((2, segments * unit, width), own.dtype),
            pltpu.VMEM((parts[-1].shape[0] - unit, width), own.dtype),
            pltpu.VMEM((parts[-1].shape[0] - unit, width), jnp.float32),
            pltpu.SemaphoreType.DMA((blocks, 2)),
            pltpu.SemaphoreType.DMA((len(parts) + 1,)),
        ],
        compiler_params=pltpu.CompilerParams(vmem_limit_bytes=32 * 1024 * 1024),
        cost_estimate=pl.CostEstimate(flops=0, bytes_accessed=0, transcendentals=0),
    )(info, units, own, peer, *parts, scale)


def per_device(codes, scales, cluster_ids, row_counts, route_offsets, partner_local):
    groups = lax.axis_size("groups")
    owners = lax.axis_size("blocks")
    pairs = lax.axis_size("pairs")
    group = lax.axis_index("groups")
    owner = lax.axis_index("blocks")
    pair = lax.axis_index("pairs")
    core = lax.axis_index("dims")
    blocks, rows, width = codes.shape
    inverse_root = 1.0 / math.sqrt(width * lax.axis_size("dims"))
    share = blocks * rows // pairs
    unit = share // 4
    rounds = owners // 2
    swap = [(0, 1), (1, 0)]
    line = ("groups", "blocks")

    def place(g, o):
        o = o % owners
        return g * owners + (o if g % 2 == 0 else owners - 1 - o)

    sign = jnp.where(group % 2 == 0, 1, -1)
    ring_place = jnp.where(group % 2 == 0, owner, owners - 1 - owner)

    def origins(step):
        return owners // 2 if 2 * step == owners else owners

    def moves(step, start, stop):
        return [
            (place(g, o + start), place(g, o + stop))
            for g in range(groups) for o in range(origins(step))
        ]

    def beside(at):
        return at + owners if at // owners % 2 == 0 else at - owners

    after = lax.optimization_barrier
    detour = groups % 2 == 0

    flat = codes.reshape(-1, width)

    def quarter(number):
        return lax.dynamic_slice_in_dim(flat, pair * share + number * unit, unit, 0)

    def follow(value, *others):
        return lax.optimization_barrier((value, *others))[0]

    def send(arrays, to):
        return [lax.ppermute(array, line, to) for array in arrays]

    first = [quarter(1 - core)]
    flat = follow(flat, first[0])
    first.append(quarter(core))
    second = [quarter(3 - core), quarter(2 + core)]
    peer_codes = lax.ppermute(codes, "dims", swap)
    sliced = first[0]
    first = send(first, moves(1, 0, 1))

    route_offsets = follow(route_offsets, peer_codes)
    targets = (owner + 1 + route_offsets.reshape(-1)) % owners
    named = targets * blocks + partner_local.reshape(-1)
    block_ids = jnp.arange(owners * blocks, dtype=jnp.int32)
    counted = jnp.sum((named[None, :] == block_ids[:, None]).astype(jnp.float32), axis=1)
    listed = counted
    for step in range(1, pairs):
        listed = listed + lax.ppermute(
            counted, "pairs", [(i, (i + step) % pairs) for i in range(pairs)]
        )
    note = jnp.concatenate([
        value.reshape(-1).astype(codes.dtype) for value in (scales, cluster_ids, row_counts, listed)
    ])
    note_rows = -(-note.shape[0] // (16 * width)) * 16
    note = jnp.pad(note, (0, note_rows * width - note.shape[0])).reshape(note_rows, width)
    own_listed = listed.reshape(owners, blocks).astype(jnp.int32)
    second[0] = jnp.concatenate([second[0], note], axis=0)
    ready = second[0]
    second[1] = follow(second[1], first[0])
    second = send(second, moves(1, 0, 1))

    scale_root = scales.astype(jnp.float32) * inverse_root
    units = jnp.stack([pair * 4 + core, pair * 4 + core + 2]).astype(jnp.int32)

    def exchanged(part):
        return lax.ppermute(part, "dims", swap)

    row_parts, column_parts = [], []
    others = [None, None]
    for step in range(1, rounds + 1):
        held, held_second = list(first), list(second)
        if step < rounds:
            perm = moves(step + 1, step, step + 1)
            if detour:
                aside = [(s, beside(s)) for s, _ in perm]
                home = [(beside(s), t) for s, t in perm]
                one = lax.ppermute(follow(held[0], ready), line, aside)
                two = lax.ppermute(held[1], line, aside)
                first = send([one, two], home)
            else:
                one, two = held
                first = send(held, perm)
            second[0] = lax.ppermute(follow(held_second[0], one), line, perm)
        note = held_second[0][unit:].reshape(-1)
        scale_end = blocks * rows
        cluster_end, count_end = scale_end + blocks, scale_end + 2 * blocks
        from_owner = (owner - sign * step) % owners
        active = ((ring_place - step) % owners) < origins(step)
        info = jnp.concatenate([
            cluster_ids,
            row_counts,
            lax.dynamic_index_in_dim(own_listed, from_owner, 0, keepdims=False),
            note[scale_end:count_end].astype(jnp.int32),
            lax.dynamic_slice_in_dim(note, count_end + owner * blocks, blocks, 0).astype(jnp.int32),
            active.astype(jnp.int32)[None],
        ])
        if others[0] is None:
            others[0] = exchanged(held[0])
        if others[1] is None:
            others[1] = exchanged(held_second[0])
        chunks = [held[1], others[0], follow(held_second[1], others[0], others[1], info), others[1]]
        others = [None, None]
        if step < rounds:
            others[1] = exchanged(second[0])
            info = follow(info, one)
            second[1] = lax.ppermute(held_second[1], line, perm)
        row_sums, columns = tile_sums(
            info, units, codes, peer_codes, chunks, scale_root
        )
        row_parts.append(row_sums)
        if step < rounds:
            columns = follow(columns, row_sums)
        if step < rounds or pairs != 2:
            columns = lax.ppermute(
                columns, line,
                [(place(g, o + step), place(g, o)) for g in range(groups) for o in range(owners)],
            )
            column_parts.append(columns)
        if step < rounds:
            first[0] = follow(first[0], row_sums)
            first[1], second[1] = follow(first[1], columns), follow(second[1], columns)
    cores = jnp.arange(2)[None, :] == core
    here = (jnp.arange(pairs)[:, None] == pair) & cores
    density = sum(row_parts)
    if column_parts:
        density = density + jnp.where(
            here[:, None, :, None], sum(column_parts)[None, :, None, :], 0.0
        ).reshape(blocks, rows)
    if pairs != 2:
        return jnp.log1p(lax.psum(density, ("pairs", "dims")))
    outgoing = jnp.where(cores[:, :, None], columns[:, None, :], 0.0).reshape(-1, rows)
    both = jnp.concatenate([density, outgoing], axis=0)
    both = both + lax.ppermute(both, "dims", swap)
    density, outgoing = both[:blocks], both[blocks:]
    across = [(0, 1), (1, 0)]
    joint = ("groups", "blocks", "pairs")
    back = [
        (place(g, o + rounds) * 2 + p, place(g, o) * 2, p)
        for g in range(groups) for o in range(owners) for p in range(2)
    ]
    parts = [
        lax.ppermute(density, "pairs", across),
        lax.ppermute(outgoing, joint, [(s, t + p) for s, t, p in back]),
        lax.ppermute(outgoing, joint, [(s, t + 1 - p) for s, t, p in back]),
    ]
    straight, crossed = parts[1].reshape(1, -1, rows), parts[2].reshape(1, -1, rows)
    own_pair = (jnp.arange(2) == pair)[:, None, None]
    columns = jnp.where(own_pair, straight, crossed).reshape(blocks, rows)
    return jnp.log1p(density + parts[0] + columns)


def solution(mesh):
    return jax.shard_map(
        per_device,
        mesh=mesh,
        in_specs=(
            P(("groups", "blocks"), None, "dims"),
            P(("groups", "blocks"), None),
            P(("groups", "blocks")),
            P(("groups", "blocks")),
            P(("groups", "blocks"), "pairs", None, None),
            P(("groups", "blocks"), "pairs", None),
        ),
        out_specs=P(("groups", "blocks"), None),
        check_vma=False,
    )
```

```python
import functools
import math

import jax
import jax.numpy as jnp
from jax import lax
from jax.experimental import pallas as pl
from jax.experimental.pallas import tpu as pltpu
from jax.sharding import PartitionSpec as P

NT = (((1,), (1,)), ((), ()))
LANES = 128
LOG2E = math.log2(math.e)


def tile_kernel(info_ref, units_ref, own_ref, peer_ref, *refs):
    count = len(refs) - 11
    parts = refs[:count]
    (scale_ref, rows_ref, columns_ref, held_ref, total_ref, wide_ref, part_ref, raw_ref, note_ref,
     copied, part_copied) = refs[count:]
    blocks, rows, width = own_ref.shape
    segments, unit = columns_ref.shape

    def copies(block):
        return [
            pltpu.make_async_copy(whole.at[block], held_ref.at[block, half], copied.at[block, half])
            for half, whole in enumerate((own_ref, peer_ref))
        ]

    note_rows = parts[-1].shape[0] - unit
    part_copies = [
        pltpu.make_async_copy(
            part.at[pl.ds(0, unit)], part_ref.at[i % 2, pl.ds(i // 2 * unit, unit)], part_copied.at[i]
        )
        for i, part in enumerate(parts)
    ]
    part_copies.append(pltpu.make_async_copy(
        parts[-1].at[pl.ds(unit, note_rows)], raw_ref, part_copied.at[count]
    ))
    for copy in part_copies:
        copy.start()
    valid, weights = [], []
    for segment in range(segments):
        first_row = units_ref[segment] * unit
        part_block = first_row // rows
        left = info_ref[4 * blocks + part_block] - (first_row - part_block * rows)
        valid.append(left)
        weights.append([
            jnp.where(
                (info_ref[3 * blocks + part_block] == info_ref[block]) & (left > 0),
                info_ref[2 * blocks + part_block] + info_ref[5 * blocks + block],
                0,
            ) * info_ref[6 * blocks]
            for block in range(blocks)
        ])
    needed = [sum(weights[segment][block] for segment in range(segments)) for block in range(blocks)]
    for block in range(blocks):

        @pl.when(needed[block] != 0)
        def _(block=block):
            for copy in copies(block):
                copy.start()

    rows_ref[...] = jnp.zeros_like(rows_ref)
    total_ref[...] = jnp.zeros_like(total_ref)
    for copy in part_copies:
        copy.wait()
    note_ref[...] = raw_ref[...].astype(jnp.float32)
    in_row = width // unit
    for segment in range(segments):
        line = note_ref[pl.ds(units_ref[segment] // in_row, 1), :]
        at = units_ref[segment] % in_row
        part_scale = line[:, :unit]
        for i in range(1, in_row):
            part_scale = jnp.where(at == i, line[:, i * unit : (i + 1) * unit], part_scale)
        wide_ref[0, segment] = jnp.transpose(jnp.broadcast_to(part_scale, (LANES, unit)))
        row_ids = lax.broadcasted_iota(jnp.int32, (unit, LANES), 0)
        wide_ref[1, segment] = (row_ids < valid[segment]).astype(jnp.float32)

    def product(block, first, length):
        return sum(
            lax.dot_general(
                part_ref[half, first : first + length, :], held_ref[block, half], NT,
                preferred_element_type=jnp.float32,
            )
            for half in range(2)
        )

    def tile(segment, block, gram):
        factor = weights[segment][block].astype(jnp.float32)
        row_ids = lax.broadcasted_iota(jnp.int32, (1, LANES), 1)
        for start in range(0, rows, LANES):
            own_scale = scale_ref[block : block + 1, start : start + LANES] * LOG2E
            own_valid = jnp.where(row_ids + start < info_ref[blocks + block], factor, 0.0)
            summed = jnp.zeros((8, LANES), jnp.float32)
            for at in range(0, unit, 64):
                here = pl.ds(at, 64)
                scaled = gram[at : at + 64, start : start + LANES] * (
                    wide_ref[0, segment, here, :] * own_scale
                )
                kern = jnp.exp2(scaled) * wide_ref[1, segment, here, :]
                summed = summed + jnp.sum(kern.reshape(-1, 8, LANES), axis=0)
                total_ref[segment, here, :] += kern * own_valid
            rows_ref[block : block + 1, start : start + LANES] += own_valid * jnp.sum(
                summed, axis=0, keepdims=True
            )

    for block in range(blocks):

        @pl.when(needed[block] != 0)
        def _(block=block):
            for copy in copies(block):
                copy.wait()
            wanted = [weights[segment][block] != 0 for segment in range(segments)]
            every = functools.reduce(jnp.logical_and, wanted)

            @pl.when(every)
            def _():
                gram = product(block, 0, segments * unit)
                for segment in range(segments):
                    tile(segment, block, gram[segment * unit : (segment + 1) * unit])

            for segment in range(segments):

                @pl.when(wanted[segment] & jnp.logical_not(every))
                def _(segment=segment):
                    tile(segment, block, product(block, segment * unit, unit))

    for segment in range(segments):
        columns_ref[segment : segment + 1, :] = jnp.sum(
            jnp.transpose(total_ref[segment]), axis=0, keepdims=True
        )


def tile_sums(info, units, own, peer, parts, scale):
    blocks, rows, width = own.shape
    segments, unit = len(parts) // 2, parts[0].shape[0]
    smem = pl.BlockSpec(memory_space=pltpu.SMEM)
    vmem = pl.BlockSpec(memory_space=pltpu.VMEM)
    held = pl.BlockSpec(memory_space=pl.ANY)
    return pl.pallas_call(
        tile_kernel,
        out_shape=(
            jax.ShapeDtypeStruct((blocks, rows), jnp.float32),
            jax.ShapeDtypeStruct((segments, unit), jnp.float32),
        ),
        in_specs=[smem, smem, held, held] + [held] * len(parts) + [vmem],
        out_specs=(vmem, vmem),
        scratch_shapes=[
            pltpu.VMEM((blocks, 2, rows, width), own.dtype),
            pltpu.VMEM((segments, unit, LANES), jnp.float32),
            pltpu.VMEM((2, segments, unit, LANES), jnp.float32),
            pltpu.VMEM((2, segments * unit, width), own.dtype),
            pltpu.VMEM((parts[-1].shape[0] - unit, width), own.dtype),
            pltpu.VMEM((parts[-1].shape[0] - unit, width), jnp.float32),
            pltpu.SemaphoreType.DMA((blocks, 2)),
            pltpu.SemaphoreType.DMA((len(parts) + 1,)),
        ],
        compiler_params=pltpu.CompilerParams(vmem_limit_bytes=32 * 1024 * 1024),
        cost_estimate=pl.CostEstimate(flops=0, bytes_accessed=0, transcendentals=0),
    )(info, units, own, peer, *parts, scale)


def per_device(codes, scales, cluster_ids, row_counts, route_offsets, partner_local):
    groups = lax.axis_size("groups")
    owners = lax.axis_size("blocks")
    pairs = lax.axis_size("pairs")
    group = lax.axis_index("groups")
    owner = lax.axis_index("blocks")
    pair = lax.axis_index("pairs")
    core = lax.axis_index("dims")
    blocks, rows, width = codes.shape
    inverse_root = 1.0 / math.sqrt(width * lax.axis_size("dims"))
    share = blocks * rows // pairs
    unit = share // 4
    rounds = owners // 2
    swap = [(0, 1), (1, 0)]
    line = ("groups", "blocks")

    def place(g, o):
        o = o % owners
        return g * owners + (o if g % 2 == 0 else owners - 1 - o)

    sign = jnp.where(group % 2 == 0, 1, -1)
    ring_place = jnp.where(group % 2 == 0, owner, owners - 1 - owner)

    def origins(step):
        return owners // 2 if 2 * step == owners else owners

    def moves(step, start, stop, every=False):
        return [
            (place(g, o + start), place(g, o + stop))
            for g in range(groups) for o in range(owners if every else origins(step))
        ]

    def beside(at):
        return at + owners if at // owners % 2 == 0 else at - owners

    after = lax.optimization_barrier
    detour = groups % 2 == 0

    flat = codes.reshape(-1, width)

    def quarter(number):
        return lax.dynamic_slice_in_dim(flat, pair * share + number * unit, unit, 0)

    def follow(value, *others):
        return lax.optimization_barrier((value, *others))[0]

    def send(arrays, to):
        return [lax.ppermute(array, line, to) for array in arrays]

    first = [quarter(1 - core)]
    flat = follow(flat, first[0])
    first.append(quarter(core))
    second = [quarter(3 - core), quarter(2 + core)]
    peer_codes = lax.ppermute(codes, "dims", swap)
    sliced = first[0]
    first = send(first, moves(1, 0, 1))

    route_offsets = follow(route_offsets, peer_codes)
    targets = (owner + 1 + route_offsets.reshape(-1)) % owners
    named = targets * blocks + partner_local.reshape(-1)
    block_ids = jnp.arange(owners * blocks, dtype=jnp.int32)
    counted = jnp.sum((named[None, :] == block_ids[:, None]).astype(jnp.float32), axis=1)
    listed = counted
    for step in range(1, pairs):
        listed = listed + lax.ppermute(
            counted, "pairs", [(i, (i + step) % pairs) for i in range(pairs)]
        )
    note = jnp.concatenate([
        value.reshape(-1).astype(codes.dtype) for value in (scales, cluster_ids, row_counts, listed)
    ])
    note_rows = -(-note.shape[0] // (16 * width)) * 16
    note = jnp.pad(note, (0, note_rows * width - note.shape[0])).reshape(note_rows, width)
    own_listed = listed.reshape(owners, blocks).astype(jnp.int32)
    second[0] = jnp.concatenate([second[0], note], axis=0)
    ready = second[0]
    second[1] = follow(second[1], first[0])
    second = send(second, moves(1, 0, 1))

    scale_root = scales.astype(jnp.float32) * inverse_root
    units = jnp.stack([pair * 4 + core, pair * 4 + core + 2]).astype(jnp.int32)

    def exchanged(part):
        return lax.ppermute(part, "dims", swap)

    row_parts, column_parts = [], []
    others = [None, None]
    for step in range(1, rounds + 1):
        held, held_second = list(first), list(second)
        if step < rounds:
            perm = moves(step + 1, step, step + 1)
            if detour:
                aside = [(s, beside(s)) for s, _ in perm]
                home = [(beside(s), t) for s, t in perm]
                one = lax.ppermute(follow(held[0], ready), line, aside)
                two = lax.ppermute(held[1], line, aside)
                first = send([one, two], home)
            else:
                one, two = held
                first = send(held, perm)
            second[0] = lax.ppermute(follow(held_second[0], one), line, perm)
        note = held_second[0][unit:].reshape(-1)
        scale_end = blocks * rows
        cluster_end, count_end = scale_end + blocks, scale_end + 2 * blocks
        from_owner = (owner - sign * step) % owners
        active = ((ring_place - step) % owners) < origins(step)
        info = jnp.concatenate([
            cluster_ids,
            row_counts,
            lax.dynamic_index_in_dim(own_listed, from_owner, 0, keepdims=False),
            note[scale_end:count_end].astype(jnp.int32),
            lax.dynamic_slice_in_dim(note, count_end + owner * blocks, blocks, 0).astype(jnp.int32),
            active.astype(jnp.int32)[None],
        ])
        if others[0] is None:
            others[0] = exchanged(follow(held[0], info) if step == 1 else held[0])
        if others[1] is None:
            others[1] = exchanged(held_second[0])
        last = held_second[1] if step == 1 else follow(held_second[1], others[0], others[1], info)
        chunks = [held[1], others[0], last, others[1]]
        others = [None, None]
        if step < rounds:
            others[1] = exchanged(second[0])
            info = follow(info, one)
            second[1] = lax.ppermute(held_second[1], line, perm)
        row_sums, columns = tile_sums(
            info, units, codes, peer_codes, chunks, scale_root
        )
        row_parts.append(row_sums)
        if step < rounds:
            columns = follow(columns, row_sums)
        if step < rounds or pairs != 2:
            columns = lax.ppermute(
                columns, line,
                [(place(g, o + step), place(g, o)) for g in range(groups) for o in range(owners)],
            )
            column_parts.append(columns)
        if step < rounds:
            first[0] = follow(first[0], row_sums)
            first[1], second[1] = follow(first[1], columns), follow(second[1], columns)
    cores = jnp.arange(2)[None, :] == core
    here = (jnp.arange(pairs)[:, None] == pair) & cores
    density = sum(row_parts)
    if column_parts:
        density = density + jnp.where(
            here[:, None, :, None], sum(column_parts)[None, :, None, :], 0.0
        ).reshape(blocks, rows)
    if pairs != 2:
        return jnp.log1p(lax.psum(density, ("pairs", "dims")))
    outgoing = jnp.where(cores[:, :, None], columns[:, None, :], 0.0).reshape(-1, rows)
    both = jnp.concatenate([density, outgoing], axis=0)
    both = both + lax.ppermute(both, "dims", swap)
    density, outgoing = both[:blocks], both[blocks:]
    across = [(0, 1), (1, 0)]
    both = lax.ppermute(both, "pairs", across)
    density = density + both[:blocks]
    other = both[blocks:].reshape(1, -1, rows)
    outgoing = outgoing.reshape(1, -1, rows)
    own_pair = (jnp.arange(2) == pair)[:, None, None]
    columns = lax.ppermute(
        jnp.where(own_pair, outgoing, other), line, moves(rounds, rounds, 0, True)
    )
    return jnp.log1p(density + columns.reshape(blocks, rows))


def solution(mesh):
    return jax.shard_map(
        per_device,
        mesh=mesh,
        in_specs=(
            P(("groups", "blocks"), None, "dims"),
            P(("groups", "blocks"), None),
            P(("groups", "blocks")),
            P(("groups", "blocks")),
            P(("groups", "blocks"), "pairs", None, None),
            P(("groups", "blocks"), "pairs", None),
        ),
        out_specs=P(("groups", "blocks"), None),
        check_vma=False,
    )
```

```python
import functools
import math

import jax
import jax.numpy as jnp
from jax import lax
from jax.experimental import pallas as pl
from jax.experimental.pallas import tpu as pltpu
from jax.sharding import PartitionSpec as P

NT = (((1,), (1,)), ((), ()))
LANES = 128
LOG2E = math.log2(math.e)


def tile_kernel(info_ref, units_ref, own_ref, peer_ref, *refs):
    count = len(refs) - 11
    parts = refs[:count]
    (scale_ref, rows_ref, columns_ref, held_ref, total_ref, wide_ref, part_ref, raw_ref, note_ref,
     copied, part_copied) = refs[count:]
    blocks, rows, width = own_ref.shape
    segments, unit = columns_ref.shape

    def copies(block):
        return [
            pltpu.make_async_copy(whole.at[block], held_ref.at[block, half], copied.at[block, half])
            for half, whole in enumerate((own_ref, peer_ref))
        ]

    note_rows = parts[-1].shape[0] - unit
    part_copies = [
        pltpu.make_async_copy(
            part.at[pl.ds(0, unit)], part_ref.at[i % 2, pl.ds(i // 2 * unit, unit)], part_copied.at[i]
        )
        for i, part in enumerate(parts)
    ]
    note_copy = pltpu.make_async_copy(
        parts[-1].at[pl.ds(unit, note_rows)], raw_ref, part_copied.at[count]
    )
    note_copy.start()
    for copy in part_copies:
        copy.start()
    valid, weights = [], []
    for segment in range(segments):
        first_row = units_ref[segment] * unit
        part_block = first_row // rows
        left = info_ref[4 * blocks + part_block] - (first_row - part_block * rows)
        valid.append(left)
        weights.append([
            jnp.where(
                (info_ref[3 * blocks + part_block] == info_ref[block]) & (left > 0),
                info_ref[2 * blocks + part_block] + info_ref[5 * blocks + block],
                0,
            ) * info_ref[6 * blocks]
            for block in range(blocks)
        ])
    needed = [sum(weights[segment][block] for segment in range(segments)) for block in range(blocks)]
    for block in range(blocks):

        @pl.when(needed[block] != 0)
        def _(block=block):
            for copy in copies(block):
                copy.start()

    rows_ref[...] = jnp.zeros_like(rows_ref)
    total_ref[...] = jnp.zeros_like(total_ref)
    note_copy.wait()
    note_ref[...] = raw_ref[...].astype(jnp.float32)
    in_row = width // unit
    for segment in range(segments):
        line = note_ref[pl.ds(units_ref[segment] // in_row, 1), :]
        at = units_ref[segment] % in_row
        part_scale = line[:, :unit]
        for i in range(1, in_row):
            part_scale = jnp.where(at == i, line[:, i * unit : (i + 1) * unit], part_scale)
        wide_ref[0, segment] = jnp.transpose(jnp.broadcast_to(part_scale, (LANES, unit)))
        row_ids = lax.broadcasted_iota(jnp.int32, (unit, LANES), 0)
        wide_ref[1, segment] = (row_ids < valid[segment]).astype(jnp.float32)
    for copy in part_copies:
        copy.wait()

    def product(block, first, length, used):
        return sum(
            lax.dot_general(
                part_ref[half, first : first + length, :], held_ref[block, half, :used, :], NT,
                preferred_element_type=jnp.float32,
            )
            for half in range(2)
        )

    def tile(segment, block, gram):
        factor = weights[segment][block].astype(jnp.float32)
        row_ids = lax.broadcasted_iota(jnp.int32, (1, LANES), 1)
        for start in range(0, gram.shape[1], LANES):
            own_scale = scale_ref[block : block + 1, start : start + LANES] * LOG2E
            own_valid = jnp.where(row_ids + start < info_ref[blocks + block], factor, 0.0)
            summed = jnp.zeros((8, LANES), jnp.float32)
            for at in range(0, unit, 64):
                here = pl.ds(at, 64)
                scaled = gram[at : at + 64, start : start + LANES] * (
                    wide_ref[0, segment, here, :] * own_scale
                )
                kern = jnp.exp2(scaled) * wide_ref[1, segment, here, :]
                summed = summed + jnp.sum(kern.reshape(-1, 8, LANES), axis=0)
                total_ref[segment, here, :] += kern * own_valid
            rows_ref[block : block + 1, start : start + LANES] += own_valid * jnp.sum(
                summed, axis=0, keepdims=True
            )

    for block in range(blocks):

        @pl.when(needed[block] != 0)
        def _(block=block):
            for copy in copies(block):
                copy.wait()
            wanted = [weights[segment][block] != 0 for segment in range(segments)]
            every = functools.reduce(jnp.logical_and, wanted)
            few = info_ref[blocks + block] <= rows // 2
            for used, fits in ((rows // 2, few), (rows, jnp.logical_not(few))):

                @pl.when(every & fits)
                def _(used=used):
                    gram = product(block, 0, segments * unit, used)
                    for segment in range(segments):
                        tile(segment, block, gram[segment * unit : (segment + 1) * unit])

                for segment in range(segments):

                    @pl.when(wanted[segment] & jnp.logical_not(every) & fits)
                    def _(segment=segment, used=used):
                        tile(segment, block, product(block, segment * unit, unit, used))

    for segment in range(segments):
        columns_ref[segment : segment + 1, :] = jnp.sum(
            jnp.transpose(total_ref[segment]), axis=0, keepdims=True
        )


def tile_sums(info, units, own, peer, parts, scale):
    blocks, rows, width = own.shape
    segments, unit = len(parts) // 2, parts[0].shape[0]
    smem = pl.BlockSpec(memory_space=pltpu.SMEM)
    vmem = pl.BlockSpec(memory_space=pltpu.VMEM)
    held = pl.BlockSpec(memory_space=pl.ANY)
    return pl.pallas_call(
        tile_kernel,
        out_shape=(
            jax.ShapeDtypeStruct((blocks, rows), jnp.float32),
            jax.ShapeDtypeStruct((segments, unit), jnp.float32),
        ),
        in_specs=[smem, smem, held, held] + [held] * len(parts) + [vmem],
        out_specs=(vmem, vmem),
        scratch_shapes=[
            pltpu.VMEM((blocks, 2, rows, width), own.dtype),
            pltpu.VMEM((segments, unit, LANES), jnp.float32),
            pltpu.VMEM((2, segments, unit, LANES), jnp.float32),
            pltpu.VMEM((2, segments * unit, width), own.dtype),
            pltpu.VMEM((parts[-1].shape[0] - unit, width), own.dtype),
            pltpu.VMEM((parts[-1].shape[0] - unit, width), jnp.float32),
            pltpu.SemaphoreType.DMA((blocks, 2)),
            pltpu.SemaphoreType.DMA((len(parts) + 1,)),
        ],
        compiler_params=pltpu.CompilerParams(vmem_limit_bytes=32 * 1024 * 1024),
        cost_estimate=pl.CostEstimate(flops=0, bytes_accessed=0, transcendentals=0),
    )(info, units, own, peer, *parts, scale)


def per_device(codes, scales, cluster_ids, row_counts, route_offsets, partner_local):
    groups = lax.axis_size("groups")
    owners = lax.axis_size("blocks")
    pairs = lax.axis_size("pairs")
    group = lax.axis_index("groups")
    owner = lax.axis_index("blocks")
    pair = lax.axis_index("pairs")
    core = lax.axis_index("dims")
    blocks, rows, width = codes.shape
    inverse_root = 1.0 / math.sqrt(width * lax.axis_size("dims"))
    share = blocks * rows // pairs
    unit = share // 4
    rounds = owners // 2
    swap = [(0, 1), (1, 0)]
    line = ("groups", "blocks")

    def place(g, o):
        o = o % owners
        return g * owners + (o if g % 2 == 0 else owners - 1 - o)

    sign = jnp.where(group % 2 == 0, 1, -1)
    ring_place = jnp.where(group % 2 == 0, owner, owners - 1 - owner)

    def origins(step):
        return owners // 2 if 2 * step == owners else owners

    def moves(step, start, stop, every=False):
        return [
            (place(g, o + start), place(g, o + stop))
            for g in range(groups) for o in range(owners if every else origins(step))
        ]

    def beside(at):
        return at + owners if at // owners % 2 == 0 else at - owners

    after = lax.optimization_barrier
    detour = groups % 2 == 0

    flat = codes.reshape(-1, width)

    def quarter(number):
        return lax.dynamic_slice_in_dim(flat, pair * share + number * unit, unit, 0)

    def follow(value, *others):
        return lax.optimization_barrier((value, *others))[0]

    def send(arrays, to):
        return [lax.ppermute(array, line, to) for array in arrays]

    first = [quarter(1 - core)]
    flat = follow(flat, first[0])
    first.append(quarter(core))
    second = [quarter(3 - core), quarter(2 + core)]
    peer_codes = lax.ppermute(codes, "dims", swap)
    sliced = first[0]
    first = send(first, moves(1, 0, 1))

    route_offsets = follow(route_offsets, peer_codes)
    targets = (owner + 1 + route_offsets.reshape(-1)) % owners
    named = targets * blocks + partner_local.reshape(-1)
    block_ids = jnp.arange(owners * blocks, dtype=jnp.int32)
    counted = jnp.sum((named[None, :] == block_ids[:, None]).astype(jnp.float32), axis=1)
    listed = counted
    for step in range(1, pairs):
        listed = listed + lax.ppermute(
            counted, "pairs", [(i, (i + step) % pairs) for i in range(pairs)]
        )
    note = jnp.concatenate([
        value.reshape(-1).astype(codes.dtype) for value in (scales, cluster_ids, row_counts, listed)
    ])
    note_rows = -(-note.shape[0] // (16 * width)) * 16
    note = jnp.pad(note, (0, note_rows * width - note.shape[0])).reshape(note_rows, width)
    own_listed = listed.reshape(owners, blocks).astype(jnp.int32)
    second[0] = jnp.concatenate([second[0], note], axis=0)
    ready = second[0]
    second[1] = follow(second[1], first[0])
    second = send(second, moves(1, 0, 1))

    scale_root = scales.astype(jnp.float32) * inverse_root
    units = jnp.stack([pair * 4 + core, pair * 4 + core + 2]).astype(jnp.int32)

    def exchanged(part):
        return lax.ppermute(part, "dims", swap)

    row_parts, column_parts = [], []
    others = [None, None]
    for step in range(1, rounds + 1):
        held, held_second = list(first), list(second)
        if step < rounds:
            perm = moves(step + 1, step, step + 1)
            if detour:
                aside = [(s, beside(s)) for s, _ in perm]
                home = [(beside(s), t) for s, t in perm]
                one = lax.ppermute(follow(held[0], ready), line, aside)
                two = lax.ppermute(held[1], line, aside)
                first = send([one, two], home)
            else:
                one, two = held
                first = send(held, perm)
            second[0] = lax.ppermute(follow(held_second[0], one), line, perm)
        note = held_second[0][unit:].reshape(-1)
        scale_end = blocks * rows
        cluster_end, count_end = scale_end + blocks, scale_end + 2 * blocks
        from_owner = (owner - sign * step) % owners
        active = ((ring_place - step) % owners) < origins(step)
        info = jnp.concatenate([
            cluster_ids,
            row_counts,
            lax.dynamic_index_in_dim(own_listed, from_owner, 0, keepdims=False),
            note[scale_end:count_end].astype(jnp.int32),
            lax.dynamic_slice_in_dim(note, count_end + owner * blocks, blocks, 0).astype(jnp.int32),
            active.astype(jnp.int32)[None],
        ])
        if others[0] is None:
            others[0] = exchanged(follow(held[0], info) if step == 1 else held[0])
        if others[1] is None:
            others[1] = exchanged(held_second[0])
        last = held_second[1] if step == 1 else follow(held_second[1], others[0], others[1], info)
        chunks = [held[1], others[0], last, others[1]]
        others = [None, None]
        if step < rounds:
            others[1] = exchanged(second[0])
            info = follow(info, one)
            second[1] = lax.ppermute(held_second[1], line, perm)
        row_sums, columns = tile_sums(
            info, units, codes, peer_codes, chunks, scale_root
        )
        row_parts.append(row_sums)
        if step < rounds:
            columns = follow(columns, row_sums)
        if step < rounds or pairs != 2:
            columns = lax.ppermute(
                columns, line,
                [(place(g, o + step), place(g, o)) for g in range(groups) for o in range(owners)],
            )
            column_parts.append(columns)
        if step < rounds:
            first[0] = follow(first[0], row_sums)
            first[1], second[1] = follow(first[1], columns), follow(second[1], columns)
    cores = jnp.arange(2)[None, :] == core
    here = (jnp.arange(pairs)[:, None] == pair) & cores
    density = sum(row_parts)
    if column_parts:
        density = density + jnp.where(
            here[:, None, :, None], sum(column_parts)[None, :, None, :], 0.0
        ).reshape(blocks, rows)
    if pairs != 2:
        return jnp.log1p(lax.psum(density, ("pairs", "dims")))
    outgoing = jnp.where(cores[:, :, None], columns[:, None, :], 0.0).reshape(-1, rows)
    both = jnp.concatenate([density, outgoing], axis=0)
    both = both + lax.ppermute(both, "dims", swap)
    density, outgoing = both[:blocks], both[blocks:]
    across = [(0, 1), (1, 0)]
    both = lax.ppermute(both, "pairs", across)
    density = density + both[:blocks]
    other = both[blocks:].reshape(1, -1, rows)
    outgoing = outgoing.reshape(1, -1, rows)
    own_pair = (jnp.arange(2) == pair)[:, None, None]
    columns = lax.ppermute(
        jnp.where(own_pair, outgoing, other), line, moves(rounds, rounds, 0, True)
    )
    return jnp.log1p(density + columns.reshape(blocks, rows))


def solution(mesh):
    return jax.shard_map(
        per_device,
        mesh=mesh,
        in_specs=(
            P(("groups", "blocks"), None, "dims"),
            P(("groups", "blocks"), None),
            P(("groups", "blocks")),
            P(("groups", "blocks")),
            P(("groups", "blocks"), "pairs", None, None),
            P(("groups", "blocks"), "pairs", None),
        ),
        out_specs=P(("groups", "blocks"), None),
        check_vma=False,
    )
```
